512 devices in a mesh: pool: 4 (over y_hi, core), grp: 32 (over z, x), tp: 4 (over y_lo).
Axes of the slice: x: 4, y: 8 (y_hi: 2, y_lo: 4; y = y_hi * 4 + y_lo), z: 8, core: 2. Of those that a mesh axis runs over, the one named last changes fastest.
Arguments:
- history: bfloat16 [32768, 3584], P(('grp', 'tp')), may hold values from -60 to 60
- norm_gain: float32 [3584], replicated, may hold values from 0.5 to 2
- key_value_weight: bfloat16 [3584, 1024], P('tp', 'pool'), may hold values from -0.09375 to 0.09375
- query_weight: bfloat16 [3584, 3584], P('tp', 'pool'), may hold values from -0.09375 to 0.09375
- live_count: int32 [4096], P(('grp', 'tp')), may hold values from 1 to 8
- owner_group: int32 [4096, 1], P(('grp', 'tp')), may hold values from 0 to 31; in each aligned block of 32 rows (0 to 31, 32 to 63, ...) at most 2 rows name the same one
- code_table: bfloat16 [512, 3584], P('pool', 'tp'), may hold values from -60 to 60
- code_ids: int32 [4, 4096], P(None, 'grp'), may hold values from 0 to 511
- key_value_cache: bfloat16 [4096, 16, 1024], P(('grp', 'tp'), None, 'pool'), may hold values from -700 to 700
Outputs:
- attended: bfloat16 [4, 4096, 3584], P(None, ('grp', 'tp'), 'pool')
- fresh_blocks: bfloat16 [32, 4, 32, 2, 8, 1024], P('grp', 'tp', None, None, None, 'pool')
The draws below stay inside these ranges and needn't reach their ends.
Inputs may be any that keep to these rules, and one draw needn't show every extreme that they name: `owner_group`: among the 32 blocks of one device no owner group is named more than 2 times, and some device names some group exactly 2 times.
All inputs are finite; a program needn't handle non-finite values.
Results may differ from the reference program's by a relative error of at most 0.02705.
Values may be sent and summed in bfloat16 or wider, within the bound.
No kernel may reach another device: no remote copies, remote signals or barrier semaphores. Data moves between devices by JAX's collectives and lax.ppermute only.
A program may use at most 64 MiB of HBM per device.

```python
import math
import jax
import jax.numpy as jnp
import numpy as np
from jax import lax

MODEL_WIDTH = 3584
QUERY_HEADS = 28
KEY_VALUE_HEADS = 4
HEAD_SIZE = 128
VOCAB = 512
DECODE_STEPS = 4
BLK = 8
NB = 32
CACHED_LENGTH = 16
CAP = 2
NBLK = 4096
ROWS = 32768
DECODE_REQUESTS = 4096
N_GRP = 32
N_TP = 4


def scaled_rows(key, rows, cols):
    first = jax.random.fold_in(key, 0)
    value_rows = jnp.clip(jax.random.normal(first, (rows, cols)), -6.0, 6.0)
    return value_rows.astype(jnp.bfloat16)


def draw_history(key, part):
    key = jax.random.fold_in(key, 11)
    return scaled_rows(key, ROWS, MODEL_WIDTH)


def draw_code_table(key, part):
    key = jax.random.fold_in(key, 12)
    return scaled_rows(key, VOCAB, MODEL_WIDTH)


def draw_key_value_cache(key, part):
    key = jax.random.fold_in(key, 13)
    first = jax.random.fold_in(key, 0)
    array_shape = (DECODE_REQUESTS, CACHED_LENGTH, KEY_VALUE_HEADS, 2, HEAD_SIZE)
    value_rows = jnp.clip(jax.random.normal(first, array_shape), -6.0, 6.0)
    return value_rows.reshape(DECODE_REQUESTS, CACHED_LENGTH, KEY_VALUE_HEADS * 2 * HEAD_SIZE).astype(jnp.bfloat16)


def touch_ends(entries, rng, least, largest):
    spot = [jax.random.randint(jax.random.fold_in(rng, axis), (), 0, length) for axis, length in enumerate(entries.shape)]
    widest = entries.shape.index(max(entries.shape))
    neighbour = spot[:widest] + [(spot[widest] + 1) % entries.shape[widest]] + spot[widest + 1:]
    return entries.at[tuple(spot)].set(least).at[tuple(neighbour)].set(largest)


def block_scale(own_key, shape, shards, low, top_value):
    gain, own = 1.0, jax.random.fold_in(own_key, 6)
    for axis_at, shards_of in shards:
        steps = jnp.exp(jax.random.uniform(jax.random.fold_in(own, axis_at), (shards_of,), jnp.float32, low / len(shards), top_value / len(shards)))
        gain = gain * jnp.repeat(steps, shape[axis_at] // shards_of).reshape([-1 if axis == axis_at else 1 for axis in range(len(shape))])
    return gain


def shared_out(key, own, number, rows, number_of, top, reach, skew):
    order = jax.random.permutation(key, number_of)
    crowded, common = portions_of(number_of, rows * top, reach, skew, True), portions_of(number_of, rows * top, reach, skew, False)
    places = jnp.arange(number_of)

    def named(sizes, offset_by):
        used = int((sizes > 0).sum())
        fixed = max(1, used // 4)
        passed = fixed + (places - fixed + offset_by * (used - fixed)) % max(1, number_of - fixed)
        return jnp.zeros((number_of,), jnp.int32).at[order[jnp.where(places < fixed, places, passed)]].set(jnp.asarray(sizes, jnp.int32))

    sizes = jnp.where(number % 4 == 0, named(crowded, number // 4), named(common, number - number // 4 - 1))
    mixed = jax.random.permutation(jax.random.fold_in(own, 3), number_of)
    source_of, sink = mixed[0:number_of // 2 * 2:2], mixed[1:number_of // 2 * 2:2]
    margin = jnp.minimum(sizes[source_of] - 1, reach - sizes[sink]) // 2
    margin = jnp.where((source_of == order[0]) | (sink == order[0]) | (sizes[sink] == 0), 0, jnp.maximum(margin, 0))
    passed = jax.random.randint(jax.random.fold_in(own, 4), (number_of // 2,), 0, 1 << 20) % (margin + 1)
    sizes = sizes.at[source_of].add(-passed).at[sink].add(passed)
    members = jnp.searchsorted(jnp.cumsum(sizes), jnp.arange(rows * top), side="right").astype(jnp.int32)
    grid = members.reshape(top, rows).T
    grid = grid[jax.random.permutation(jax.random.fold_in(own, 1), rows)]
    offset_by = jax.random.randint(jax.random.fold_in(own, 2), (rows, 1), 0, top)
    return jnp.take_along_axis(grid, (jnp.arange(top)[None, :] + offset_by) % top, axis=1)


def portions_of(number_of, total, reach, skew, full):
    loads = [(1 << 20) // math.isqrt(rank ** skew) + 1 for rank in range(1, number_of + 1)]
    largest = reach if full else min(reach, max(-(-total // number_of), total * loads[0] // sum(loads)))
    least = 1 if total - largest >= number_of - 1 else 0
    holding, surplus = [largest] + [least] * (number_of - 1), total - largest - least * (number_of - 1)
    while surplus > 0:
        free = [i for i in range(1, number_of) if holding[i] < largest] or [i for i in range(1, number_of) if holding[i] < reach]
        whole, remaining = sum([loads[i] for i in free]), surplus
        for i in free:
            addition = min(reach - holding[i], max(1, remaining * loads[i] // whole), surplus)
            holding[i] = holding[i] + addition
            surplus = surplus - addition
    return np.array(holding)


def bell_draw(rng, shape, spread, most, cuts=(), kind=jnp.bfloat16):
    drawn = jax.random.normal(rng, shape, jnp.float32) * spread
    if len(cuts) > 0:
        drawn = block_scale(rng, shape, cuts, -0.22, 0.18) * drawn
    return jnp.clip(drawn, min=-most, max=most).astype(kind)


def setup_inputs(seed: int = 0) -> dict:
    key_list = jax.random.split(jax.random.key(seed), 10)
    history = draw_history(jax.random.fold_in(key_list[9], 71), 0)
    norm_gain = jnp.clip(jnp.exp(jax.random.uniform(key_list[1], (MODEL_WIDTH,), jnp.float32, math.log(0.5), math.log(2.0))), 0.5, 2.0)
    key_value_weight = bell_draw(key_list[2], (MODEL_WIDTH, KEY_VALUE_HEADS * 2 * HEAD_SIZE), MODEL_WIDTH ** -0.5, 0.09375, ((0, 4), (1, 4)))
    query_weight = bell_draw(key_list[3], (MODEL_WIDTH, QUERY_HEADS * HEAD_SIZE), MODEL_WIDTH ** -0.5, 0.09375, ((0, 4), (1, 4)))
    live_count = touch_ends(jax.random.randint(key_list[4], (NBLK,), 1, BLK + 1), jax.random.fold_in(key_list[4], 1), 1, BLK).astype(jnp.int32)
    owner_group_keys = jax.random.split(jax.random.fold_in(key_list[5], 1), NBLK // NB)
    owner_group_turns = jax.random.permutation(jax.random.fold_in(key_list[5], 3), NBLK // NB)
    owner_group = jax.vmap(lambda own, number: shared_out(jax.random.fold_in(key_list[5], 2), own, number, NB, N_GRP, 1, CAP, 2))(owner_group_keys, owner_group_turns).reshape((NBLK, 1))
    code_table = draw_code_table(jax.random.fold_in(key_list[9], 71), 0)
    code_ids = touch_ends(jax.random.randint(key_list[7], (DECODE_STEPS, DECODE_REQUESTS), 0, VOCAB), jax.random.fold_in(key_list[7], 1), 0, VOCAB - 1).astype(jnp.int32)
    key_value_cache = draw_key_value_cache(jax.random.fold_in(key_list[9], 71), 0)
    return dict(history=history, norm_gain=norm_gain, key_value_weight=key_value_weight, query_weight=query_weight, live_count=live_count, owner_group=owner_group, code_table=code_table, code_ids=code_ids, key_value_cache=key_value_cache)


EPSILON = 1e-06

def row_scale(value_rows):
    return lax.rsqrt(lax.optimization_barrier(jnp.mean(value_rows * value_rows, axis=-1, keepdims=True)) + EPSILON)

def reference(history, norm_gain, key_value_weight, query_weight, live_count, owner_group, code_table, code_ids, key_value_cache):
    key_value_width = KEY_VALUE_HEADS * 2 * HEAD_SIZE
    hist_f32 = history.astype(jnp.float32)
    hist_normed = (hist_f32 * norm_gain).astype(jnp.bfloat16)
    hist_kv = (row_scale(hist_f32) * jnp.dot(hist_normed, key_value_weight, preferred_element_type=jnp.float32)).astype(jnp.bfloat16)
    blocks = hist_kv.reshape(NBLK, BLK, key_value_width)
    keep = jnp.arange(BLK, dtype=jnp.int32)[None, :] < live_count[:, None]
    blocks = jnp.where(keep[:, :, None], blocks, jnp.zeros_like(blocks))
    senders = N_GRP * N_TP
    target = owner_group[:, 0].reshape(senders, NB)
    same_target = target[:, :, None] == target[:, None, :]
    order = jnp.arange(NB, dtype=jnp.int32)
    earlier = order[None, :] < order[:, None]
    rank = lax.optimization_barrier(jnp.sum((same_target & earlier[None]).astype(jnp.int32), axis=2))
    groups = jnp.arange(N_GRP, dtype=jnp.int32)
    slots = jnp.arange(CAP, dtype=jnp.int32)
    select = ((target[:, None, None, :] == groups[None, :, None, None]) & (rank[:, None, None, :] == slots[None, None, :, None])).astype(jnp.float32)
    flat_blocks = blocks.reshape(senders, NB, BLK * key_value_width).astype(jnp.float32)
    moved = jnp.einsum('sgkb,sbx->gskx', select, flat_blocks)
    moved = moved.reshape(N_GRP, N_GRP, N_TP, CAP, BLK, key_value_width).transpose(0, 2, 1, 3, 4, 5)
    fresh_blocks = moved.astype(jnp.bfloat16)
    request_list = code_ids.shape[1]
    heads_per_group = QUERY_HEADS // KEY_VALUE_HEADS
    tokens = jnp.take(code_table, code_ids.reshape(-1), axis=0)
    tok_f32 = tokens.astype(jnp.float32)
    tok_scale = row_scale(tok_f32)
    tok_normed = (tok_f32 * norm_gain).astype(jnp.bfloat16)
    query_rows = (tok_scale * jnp.dot(tok_normed, query_weight, preferred_element_type=jnp.float32)).astype(jnp.bfloat16)
    fresh_key_value = (tok_scale * jnp.dot(tok_normed, key_value_weight, preferred_element_type=jnp.float32)).astype(jnp.bfloat16)
    query_rows = query_rows.reshape(DECODE_STEPS, request_list, KEY_VALUE_HEADS, heads_per_group, HEAD_SIZE).astype(jnp.float32)
    fresh_key_value = fresh_key_value.reshape(DECODE_STEPS, request_list, KEY_VALUE_HEADS, 2, HEAD_SIZE)
    cached_entries = key_value_cache.reshape(request_list, CACHED_LENGTH, KEY_VALUE_HEADS, 2, HEAD_SIZE)
    keys = jnp.concatenate([cached_entries[:, :, :, 0], fresh_key_value[:, :, :, 0].transpose(1, 0, 2, 3)], axis=1).astype(jnp.float32)
    value_rows = jnp.concatenate([cached_entries[:, :, :, 1], fresh_key_value[:, :, :, 1].transpose(1, 0, 2, 3)], axis=1).astype(jnp.float32)
    scores = jnp.einsum('srhqd,rkhd->srhqk', query_rows, keys) / math.sqrt(HEAD_SIZE)
    steps_idx = jnp.arange(DECODE_STEPS, dtype=jnp.int32)
    new_allowed = steps_idx[None, :] <= steps_idx[:, None]
    allowed = jnp.concatenate([jnp.ones((DECODE_STEPS, CACHED_LENGTH), dtype=bool), new_allowed], axis=1)
    allowed = allowed[:, None, None, None, :]
    top = lax.optimization_barrier(jnp.max(jnp.where(allowed, scores, -1e+30), axis=-1, keepdims=True))
    weights = jnp.where(allowed, jnp.exp(scores - top), 0.0)
    total = lax.optimization_barrier(jnp.sum(weights, axis=-1, keepdims=True))
    probs = (weights / total).astype(jnp.bfloat16)
    attended = jnp.einsum('srhqk,rkhd->srhqd', probs.astype(jnp.float32), value_rows)
    attended = attended.reshape(DECODE_STEPS, request_list, QUERY_HEADS * HEAD_SIZE).astype(jnp.bfloat16)
    return (attended, fresh_blocks)
```

```python
import math

import jax
import jax.numpy as jnp
from jax import lax
from jax.sharding import Mesh, PartitionSpec as P

MODEL_WIDTH = 3584
HEAD_SIZE = 128
EPSILON = 1e-06
BF16 = jnp.bfloat16
F32 = jnp.float32


def spread(x, axes, number):
    copies = jnp.broadcast_to(x[None], (number,) + x.shape)
    return lax.all_to_all(copies, axes, 0, 0, tiled=True)


def code_projection(table, gain_part, query_weight, key_value_weight):
    z, x = lax.axis_index("z"), lax.axis_index("x")
    groups = lax.axis_size("z") * lax.axis_size("x")
    cores, halves = lax.axis_size("core"), lax.axis_size("yh")
    local_codes = table.shape[0]
    share = local_codes // groups
    group = z * lax.axis_size("x") + x
    mine = lax.dynamic_slice_in_dim(table, group * share, share)
    rows = spread(mine, ("yh", "core"), halves * cores).reshape(halves * cores * share, -1)
    rows_f32 = rows.astype(F32)
    square = jnp.sum(rows_f32 * rows_f32, axis=-1, keepdims=True)
    normed = (rows_f32 * gain_part).astype(BF16)
    part = jnp.concatenate(
        [
            jnp.dot(normed, query_weight, preferred_element_type=F32),
            jnp.dot(normed, key_value_weight, preferred_element_type=F32),
            jnp.broadcast_to(square, (square.shape[0], HEAD_SIZE)),
        ],
        axis=1,
    )
    total = jnp.sum(spread(part, "tp", lax.axis_size("tp")), axis=0)
    scale = lax.rsqrt(total[:, -1:] / MODEL_WIDTH + EPSILON)
    projected = (scale * total[:, :-HEAD_SIZE]).astype(BF16)
    plane = spread(projected, "z", lax.axis_size("z"))
    whole = spread(plane, "x", lax.axis_size("x"))
    xs, zs, ps, js = (
        lax.broadcasted_iota(jnp.int32, (lax.axis_size("x"), lax.axis_size("z"), halves * cores, share), d)
        for d in range(4)
    )
    codes = ps * local_codes + (zs * lax.axis_size("x") + xs) * share + js
    return whole.reshape(codes.size, -1), codes.reshape(-1)


def shards(
    history,
    norm_gain,
    key_value_weight,
    query_weight,
    live_count,
    owner_group,
    code_table,
    code_ids,
    key_value_cache,
):
    key_value_width = key_value_weight.shape[1]
    quarter = code_table.shape[1]
    gain_part = lax.dynamic_slice_in_dim(norm_gain, lax.axis_index("tp") * quarter, quarter)
    whole_weight = spread(key_value_weight, "tp", lax.axis_size("tp")).reshape(-1, key_value_width)

    projected, codes = code_projection(code_table, gain_part, query_weight, key_value_weight)

    hist_f32 = history.astype(F32)
    hist_scale = lax.rsqrt(jnp.mean(hist_f32 * hist_f32, axis=-1, keepdims=True) + EPSILON)
    hist_normed = (hist_f32 * norm_gain).astype(BF16)
    kv_sum = jnp.dot(hist_normed, whole_weight, preferred_element_type=F32)
    hist_kv = (hist_scale * kv_sum).astype(BF16)
    blocks_here = live_count.shape[0]
    block_len = history.shape[0] // blocks_here
    groups = lax.axis_size("z") * lax.axis_size("x")
    capacity = max(2, 2 * blocks_here // groups)
    events = lax.broadcasted_iota(jnp.int32, (blocks_here, block_len), 1)
    keep = events < live_count[:, None]
    blocks = jnp.where(
        keep[:, :, None],
        hist_kv.reshape(blocks_here, block_len, key_value_width),
        jnp.zeros((), BF16),
    )
    target = owner_group[:, 0]
    same_target = target[:, None] == target[None, :]
    order = lax.iota(jnp.int32, blocks_here)
    earlier = order[None, :] < order[:, None]
    rank = jnp.sum((same_target & earlier).astype(jnp.int32), axis=1)
    group_ids = lax.iota(jnp.int32, groups)
    slot_ids = lax.iota(jnp.int32, capacity)
    select = (
        (target[None, None, :] == group_ids[:, None, None])
        & (rank[None, None, :] == slot_ids[None, :, None])
    ).astype(BF16)
    outgoing = jnp.einsum(
        "gkb,bx->gkx",
        select,
        blocks.reshape(blocks_here, block_len * key_value_width),
        preferred_element_type=F32,
    )
    outgoing = outgoing.astype(BF16).reshape(groups, capacity, block_len, key_value_width)
    received = lax.all_to_all(outgoing, ("z", "x"), 0, 0, tiled=True)
    fresh_blocks = received[None, None]

    steps = code_ids.shape[0]
    request_list = code_ids.shape[1] // lax.axis_size("tp")
    ids = lax.dynamic_slice_in_dim(code_ids, lax.axis_index("tp") * request_list, request_list, 1)
    one_hot = (ids.reshape(-1)[:, None] == codes[None, :]).astype(BF16)
    tokens = jnp.dot(one_hot, projected, preferred_element_type=F32).astype(BF16)
    heads_per_group = (tokens.shape[1] - key_value_width) // HEAD_SIZE
    query_rows = tokens[:, :-key_value_width].reshape(steps, request_list, heads_per_group, HEAD_SIZE)
    fresh_key_value = tokens[:, -key_value_width:].reshape(steps, request_list, key_value_width)
    new_keys = fresh_key_value[..., :HEAD_SIZE]
    new_values = fresh_key_value[..., HEAD_SIZE:]
    cache_keys = key_value_cache[..., :HEAD_SIZE]
    cache_values = key_value_cache[..., HEAD_SIZE:]
    inverse_root = 1.0 / math.sqrt(HEAD_SIZE)
    old_scores = (
        jnp.einsum("srqd,rcd->srqc", query_rows, cache_keys, preferred_element_type=F32)
        * inverse_root
    )
    new_scores = (
        jnp.einsum("srqd,trd->srqt", query_rows, new_keys, preferred_element_type=F32)
        * inverse_root
    )
    step_ids = lax.iota(jnp.int32, steps)
    allowed = (step_ids[None, :] <= step_ids[:, None])[:, None, None, :]
    new_masked = jnp.where(allowed, new_scores, -1e30)
    top = jnp.maximum(
        jnp.max(old_scores, axis=-1, keepdims=True), jnp.max(new_masked, axis=-1, keepdims=True)
    )
    old_weights = jnp.exp(old_scores - top)
    new_weights = jnp.where(allowed, jnp.exp(new_scores - top), 0.0)
    total = jnp.sum(old_weights, axis=-1, keepdims=True) + jnp.sum(
        new_weights, axis=-1, keepdims=True
    )
    old_probs = (old_weights / total).astype(BF16)
    new_probs = (new_weights / total).astype(BF16)
    mixed = jnp.einsum("srqc,rcd->srqd", old_probs, cache_values, preferred_element_type=F32)
    mixed = mixed + jnp.einsum("srqt,trd->srqd", new_probs, new_values, preferred_element_type=F32)
    attended = mixed.reshape(steps, request_list, heads_per_group * HEAD_SIZE).astype(BF16)
    return (attended, fresh_blocks)


def solution(mesh):
    halves, cores = 2, 2
    depth, across = 8, 4
    split = Mesh(
        mesh.devices.reshape(halves, cores, depth, across, mesh.shape["tp"]),
        ("yh", "core", "z", "x", "tp"),
    )
    pool, grp = ("yh", "core"), ("z", "x")
    rows = grp + ("tp",)
    in_specs = (
        P(rows, None),
        P(),
        P("tp", pool),
        P("tp", pool),
        P(rows),
        P(rows, None),
        P(pool, "tp"),
        P(None, grp),
        P(rows, None, pool),
    )
    out_specs = (P(None, rows, pool), P(grp, "tp", None, None, None, pool))
    return jax.shard_map(shards, mesh=split, in_specs=in_specs, out_specs=out_specs, check_vma=False)
```
